128 devices in a mesh: dp: 32 (over y, x, z_hi), pair: 4 (over z_lo, core).
Axes of the slice: x: 4, y: 4, z: 4 (z_hi: 2, z_lo: 2; z = z_hi * 2 + z_lo), core: 2. Of those that a mesh axis runs over, the one named last changes fastest.
Arguments:
- picture_embedding: bfloat16 [16384, 1152], P(('dp', 'pair')), may hold values from -15 to 15
- caption_embedding: bfloat16 [16384, 1152], P(('dp', 'pair')), may hold values from -15 to 15
- logarithmic_scale_factor: float32 [1], replicated, may hold values from 4 to 4.5
- offset_shift: float32 [1], replicated, may hold values from -7 to -5
Outputs:
- image_gradient: float32 [16384, 1152], P(('dp', 'pair'))
- text_grad: float32 [16384, 1152], P(('dp', 'pair'))
- objective_results: float32 [3], replicated
The draws below stay inside these ranges and needn't reach their ends.
All inputs are finite; a program needn't handle non-finite values.
Results may differ from the reference program's by a relative error of at most 0.0012.
Values may be sent and summed in bfloat16 or wider, within the bound.
No kernel may reach another device: no remote copies, remote signals or barrier semaphores. Data moves between devices by JAX's collectives and lax.ppermute only.
A program may use at most 128 MiB of HBM per device.

```python
import jax
import jax.numpy as jnp
from jax import lax

D = 1152
GROUP_ROWS = 512
MATCHED_EXAMPLES = 16384


def shared(key):
    direction = jax.random.normal(jax.random.fold_in(key, 101), (D,), jnp.float32)
    noise_rows = jax.random.normal(jax.random.fold_in(key, 102), (MATCHED_EXAMPLES, D), jnp.float32)
    position = jnp.arange(MATCHED_EXAMPLES).astype(jnp.float32)
    within = (jnp.arange(MATCHED_EXAMPLES) % GROUP_ROWS).astype(jnp.float32)
    fraction = 0.5 * position / MATCHED_EXAMPLES + 0.5 * within / GROUP_ROWS
    return (direction, noise_rows, fraction)


def draw_picture_embedding(key, part):
    direction, noise_rows, fraction = shared(key)
    lift_size = 0.3
    row_scale = jnp.ones((MATCHED_EXAMPLES, 1), jnp.float32)
    along = lift_size * (0.2 + 0.8 * fraction)
    values = 0.25 * row_scale * (along[:, None] * direction[None, :] + noise_rows)
    return values.astype(jnp.bfloat16)


def draw_caption_embedding(key, part):
    direction, noise_rows, fraction = shared(key)
    key = jax.random.fold_in(key, 2)
    lift_size = 0.3
    fresh_noise = jax.random.normal(key, (MATCHED_EXAMPLES, D), jnp.float32)
    row_scale = jnp.ones((MATCHED_EXAMPLES, 1), jnp.float32)
    along = lift_size * (0.2 + 0.8 * fraction)
    values = 0.25 * row_scale * (along[:, None] * direction[None, :] + 0.1 * noise_rows + fresh_noise)
    return values.astype(jnp.bfloat16)


def setup_inputs(seed: int = 0) -> dict:
    arg_keys = jax.random.split(jax.random.key(seed), 5)
    return {
        "picture_embedding": draw_picture_embedding(jax.random.fold_in(arg_keys[4], 71), 0),
        "caption_embedding": draw_caption_embedding(jax.random.fold_in(arg_keys[4], 71), 0),
        "logarithmic_scale_factor": jnp.clip(jax.random.uniform(arg_keys[2], (1,), jnp.float32, 4.0, 4.5), 4.0, 4.5),
        "offset_shift": jnp.clip(jax.random.uniform(arg_keys[3], (1,), jnp.float32, -7.0, -5.0), -7.0, -5.0),
    }


EPS = 1e-06

def normalize(embedding):
    widened = embedding.astype(jnp.float32)
    inverse = lax.rsqrt(lax.optimization_barrier(jnp.sum(widened * widened, axis=1, keepdims=True)) + EPS)
    return (widened * inverse, inverse)

def projection_helper(partial_value, unit_rows, inverse):
    radial = lax.optimization_barrier(jnp.sum(partial_value * unit_rows, axis=1, keepdims=True))
    return (partial_value - radial * unit_rows) * inverse

def reference(picture_embedding, caption_embedding, logarithmic_scale_factor, offset_shift):
    picture_entry, picture_reciprocal_length = normalize(picture_embedding)
    txt32, txt_inv = normalize(caption_embedding)
    img_unit = picture_entry.astype(jnp.bfloat16)
    caption_normalized_vectors = txt32.astype(jnp.bfloat16)
    scale_factor_current = jnp.exp(logarithmic_scale_factor[0])
    trained_offset = offset_shift[0]
    text_index = jnp.arange(MATCHED_EXAMPLES, dtype=jnp.int32)

    def block_step(totals, block_index):
        caption_piece, objective_accumulated, derivative_scale_accum, derivative_accumulated = totals
        first_row = (block_index * GROUP_ROWS).astype(jnp.int32)
        picture_examples = lax.dynamic_slice_in_dim(img_unit, first_row, GROUP_ROWS, 0)
        couple_similarity = jnp.dot(picture_examples, caption_normalized_vectors.T, preferred_element_type=jnp.float32)
        couple_similarity_raw = scale_factor_current * couple_similarity + trained_offset
        image_index = first_row + jnp.arange(GROUP_ROWS, dtype=jnp.int32)
        matched = image_index[:, None] == text_index[None, :]
        label_sign = jnp.where(matched, 1.0, -1.0).astype(jnp.float32)
        objective_accumulated = objective_accumulated + jnp.sum(jax.nn.softplus(-label_sign * couple_similarity_raw))
        pair_grads = jax.nn.sigmoid(couple_similarity_raw) - matched.astype(jnp.float32)
        derivative_scale_accum = derivative_scale_accum + jnp.sum(pair_grads * couple_similarity)
        derivative_accumulated = derivative_accumulated + jnp.sum(pair_grads)
        couple_factor_matrix = pair_grads.astype(jnp.bfloat16)
        picture_share = scale_factor_current * jnp.dot(couple_factor_matrix, caption_normalized_vectors, preferred_element_type=jnp.float32)
        caption_piece = caption_piece + scale_factor_current * jnp.dot(couple_factor_matrix.T, picture_examples, preferred_element_type=jnp.float32)
        return ((caption_piece, objective_accumulated, derivative_scale_accum, derivative_accumulated), picture_share)
    zero = jnp.zeros((), jnp.float32)
    start_totals = (jnp.zeros((MATCHED_EXAMPLES, D), jnp.float32), zero, zero, zero)
    totals, image_parts = lax.scan(block_step, start_totals, jnp.arange(MATCHED_EXAMPLES // GROUP_ROWS, dtype=jnp.int32))
    caption_piece, objective_accumulated, derivative_scale_accum, derivative_accumulated = totals
    picture_derivative_accum = image_parts.reshape(MATCHED_EXAMPLES, D)
    image_gradient = projection_helper(picture_derivative_accum, picture_entry, picture_reciprocal_length)
    text_grad = projection_helper(caption_piece, txt32, txt_inv)
    objective_results = jnp.stack([objective_accumulated / MATCHED_EXAMPLES, scale_factor_current * derivative_scale_accum / MATCHED_EXAMPLES, derivative_accumulated / MATCHED_EXAMPLES])
    return (image_gradient, text_grad, objective_results)
```

```python
import jax
import jax.numpy as jnp
from jax import lax
from jax.experimental import pallas as pl
from jax.experimental.pallas import tpu as pltpu
from jax.sharding import Mesh, PartitionSpec as P

EPS = 1e-06
AXES = ("y", "x", "zh", "zl", "c")
Z = ("zh", "zl")
Z_IMAGE = [(0, 1), (1, 0), (2, 3), (3, 2)]
Z_TEXT = [(1, 2), (2, 1), (3, 0), (0, 3)]
UP = [(i, (i + 1) % 4) for i in range(4)]
DOWN = [(i, (i - 1) % 4) for i in range(4)]
SWAP = [(0, 1), (1, 0)]
SCALE = 4.0
TILE = 256


def send(value, axis, pairs):
    return lax.ppermute(value, axis, pairs)


def normalize(embedding):
    widened = embedding.astype(jnp.float32)
    inverse = lax.rsqrt(jnp.sum(widened * widened, axis=1, keepdims=True) + EPS)
    return (widened * inverse, inverse)


def projection(total, unit_rows, inverse):
    radial = jnp.sum(total * unit_rows, axis=1, keepdims=True)
    return (total - radial * unit_rows) * inverse


def gather_ring(block, axis):
    from_down = send(block, axis, UP)
    from_up = send(block, axis, DOWN)
    half = block.shape[0] // 2
    far_first = send(from_down[:half], axis, UP)
    far_second = send(from_up[half:], axis, DOWN)
    return from_down, from_up, jnp.concatenate([far_first, far_second], axis=0)


def pair_kernel(scalars, images, texts, weights, sums):
    step = pl.program_id(0)
    temperature = scalars[0]
    offset = scalars[1]

    @pl.when(step == 0)
    def _():
        sums[...] = jnp.zeros_like(sums)

    for m in range(images.shape[0] // TILE):
        rows = pl.ds(m * TILE, TILE)
        scores = lax.dot_general(
            images[rows, :], texts[...], (((1,), (1,)), ((), ())), preferred_element_type=jnp.float32
        )
        logits = scores * temperature + offset
        small = jnp.exp(-jnp.abs(logits))
        inverse = 1.0 / (1.0 + small)
        gradient = jnp.where(logits >= 0.0, inverse, small * inverse)
        signed = logits
        if m == 0:
            row = lax.broadcasted_iota(jnp.int32, (TILE, TILE), 0)
            column = lax.broadcasted_iota(jnp.int32, (TILE, TILE), 1) + step * TILE
            matched = (row == column) & (row < 128)
            signed = jnp.where(matched, -logits, logits)
            gradient = jnp.where(matched, gradient - 1.0, gradient)
        product = small
        while product.shape[0] > 8:
            half = product.shape[0] // 2
            left, right = product[:half], product[half:]
            product = left + right + left * right
        relu = jnp.maximum(signed, 0.0)
        loss = jnp.log1p(product) + jnp.sum(relu.reshape(TILE // 8, 8, TILE), axis=0)
        slope = jnp.sum((gradient * scores).reshape(TILE // 8, 8, TILE), axis=0)
        total = jnp.sum(gradient.reshape(TILE // 8, 8, TILE), axis=0)
        sums[0] += loss
        sums[1] += slope
        sums[2] += total
        weights[rows, :] = gradient.astype(jnp.bfloat16)


def pair_weights(scalars, images, texts):
    n_images, n_texts, width = images.shape[0], texts.shape[0], images.shape[1]
    return pl.pallas_call(
        pair_kernel,
        grid=(n_texts // TILE,),
        in_specs=[
            pl.BlockSpec(memory_space=pltpu.SMEM),
            pl.BlockSpec((n_images, width), lambda j: (0, 0)),
            pl.BlockSpec((TILE, width), lambda j: (j, 0)),
        ],
        out_specs=[
            pl.BlockSpec((n_images, TILE), lambda j: (0, j)),
            pl.BlockSpec((3, 8, TILE), lambda j: (0, 0, 0)),
        ],
        out_shape=[
            jax.ShapeDtypeStruct((n_images, n_texts), jnp.bfloat16),
            jax.ShapeDtypeStruct((3, 8, TILE), jnp.float32),
        ],
        compiler_params=pltpu.CompilerParams(vmem_limit_bytes=32 * 1024 * 1024),
        cost_estimate=pl.CostEstimate(
            flops=2 * n_images * n_texts * width, bytes_accessed=8 << 20, transcendentals=2 * n_images * n_texts
        ),
    )(scalars, images, texts)


def narrow(value):
    return value.astype(jnp.float16)


def wide(value):
    return value.astype(jnp.float32)


def scatter_ring(own, low, high, far, axis):
    half = far.shape[0] // 2
    for_low = send(narrow(far[:half]), axis, DOWN)
    for_high = send(narrow(far[half:]), axis, UP)
    low = jnp.concatenate([low[:half] + wide(for_low), low[half:]], axis=0)
    high = jnp.concatenate([high[:half], high[half:] + wide(for_high)], axis=0)
    from_high = send(narrow(low), axis, DOWN)
    from_low = send(narrow(high), axis, UP)
    return own + wide(from_high) + wide(from_low)


def all_sum(value):
    for axis, pairs in (
        ("c", SWAP),
        ("x", [(0, 1), (1, 0), (2, 3), (3, 2)]),
        ("y", [(0, 1), (1, 0), (2, 3), (3, 2)]),
        (Z, Z_IMAGE),
        ("x", [(1, 2), (2, 1), (3, 0), (0, 3)]),
        ("y", [(1, 2), (2, 1), (3, 0), (0, 3)]),
        (Z, Z_TEXT),
    ):
        value = value + send(value, axis, pairs)
    return value


def per_device(picture_embedding, caption_embedding, logarithmic_scale_factor, offset_shift):
    example_number = picture_embedding.shape[0] * 128
    image32, image_inverse = normalize(picture_embedding)
    text32, text_inverse = normalize(caption_embedding)
    image = image32.astype(jnp.bfloat16)
    text = text32.astype(jnp.bfloat16)
    temperature = jnp.exp(logarithmic_scale_factor[0])
    scalars = jnp.stack([temperature, offset_shift[0]])

    image_own = jnp.concatenate([image, send(image, Z, Z_IMAGE)], axis=0)
    text_own = jnp.concatenate([text, send(text, Z, Z_TEXT)], axis=0)
    images = jnp.concatenate([image_own, *gather_ring(image_own, "x")], axis=0)
    texts_own = jnp.concatenate([text_own, *gather_ring(text_own, "y")], axis=0)
    texts = jnp.concatenate([texts_own, send(texts_own, "c", SWAP)], axis=0)

    weights, sums = pair_weights(scalars, images, texts)
    objective = all_sum(jnp.sum(sums, axis=(1, 2)).reshape(1, 3))[0]
    objective_results = objective * jnp.stack([jnp.float32(1.0), temperature, jnp.float32(1.0)]) / example_number

    block = image_own.shape[0]
    image_parts = [
        SCALE * jnp.dot(weights[i * block : (i + 1) * block], texts, preferred_element_type=jnp.float32)
        for i in range(4)
    ]

    def text_part(first):
        mine = SCALE * lax.dot_general(
            weights[:, first : first + block], images, (((0,), (0,)), ((), ())), preferred_element_type=jnp.float32
        )
        return mine

    text_parts = []
    for i in range(4):
        other = send(narrow(text_part(4 * block + i * block)), "c", SWAP)
        text_parts.append(text_part(i * block) + wide(other))

    def finish(parts, axis, pairs, unit_rows, inverse):
        total = scatter_ring(*parts, axis)
        half = block // 2
        total = total[:half] + wide(send(narrow(total[half:]), Z, pairs))
        return projection(total * (temperature / SCALE), unit_rows, inverse)

    image_gradient = finish(image_parts, "x", Z_IMAGE, image32, image_inverse)
    text_grad = finish(text_parts, "y", Z_TEXT, text32, text_inverse)
    return (image_gradient, text_grad, objective_results)


def solution(mesh):
    mesh = Mesh(mesh.devices.reshape(4, 4, 2, 2, 2), AXES)
    return jax.shard_map(
        per_device,
        mesh=mesh,
        in_specs=(P(AXES, None), P(AXES, None), P(), P()),
        out_specs=(P(AXES, None), P(AXES, None), P()),
        check_vma=False,
    )
```

```python
import functools

import jax
import jax.numpy as jnp
from jax import lax
from jax.experimental import pallas as pl
from jax.experimental.pallas import tpu as pltpu
from jax.sharding import Mesh, PartitionSpec as P

EPS = 1e-06
AXES = ("y", "x", "zh", "zl", "c")
Z = ("zh", "zl")
EVEN = [(0, 1), (1, 0), (2, 3), (3, 2)]
ODD = [(1, 2), (2, 1), (3, 0), (0, 3)]
UP = [(i, (i + 1) % 4) for i in range(4)]
DOWN = [(i, (i - 1) % 4) for i in range(4)]
SWAP = [(0, 1), (1, 0)]
SCALE = 4.0
TILE = 256
LOG2E = 1.4426950408889634
LN2 = 0.6931471805599453


def send(value, axis, pairs):
    return lax.ppermute(value, axis, pairs)


def fence(*values):
    return lax.optimization_barrier(values)


def normalize(embedding):
    widened = embedding.astype(jnp.float32)
    inverse = lax.rsqrt(jnp.sum(widened * widened, axis=1, keepdims=True) + EPS)
    return (widened * inverse, inverse)


def projection(total, unit_rows, inverse):
    radial = jnp.sum(total * unit_rows, axis=1, keepdims=True)
    return (total - radial * unit_rows) * inverse


def by_eight(value):
    return jnp.sum(value.reshape(value.shape[0] // 8, 8, value.shape[1]), axis=0)


def pair_kernel(n_images, n_texts, tiles, diagonal, scalars, *refs):
    images, texts = refs[:n_images], refs[n_images : n_images + n_texts]
    weights, sums = refs[n_images + n_texts :]
    factor = scalars[0] * LOG2E
    offset = scalars[1] * LOG2E
    totals = [jnp.zeros((8, TILE), jnp.float32) for _ in range(4)]
    for t, (i, j) in enumerate(tiles):
        scores = lax.dot_general(
            images[i][...], texts[j][...], (((1,), (1,)), ((), ())), preferred_element_type=jnp.float32
        )
        logits = scores * factor + offset
        small = jnp.exp2(-jnp.abs(logits))
        denominator = 1.0 + small
        guess = pl.reciprocal(denominator, approx=True)
        inverse = guess * (2.0 - denominator * guess)
        gradient = jnp.where(logits >= 0.0, inverse, small * inverse)
        signed = logits
        if t == diagonal:
            row = lax.broadcasted_iota(jnp.int32, (TILE, TILE), 0)
            column = lax.broadcasted_iota(jnp.int32, (TILE, TILE), 1)
            matched = (row == column) & (row < TILE // 2)
            signed = jnp.where(matched, -logits, logits)
            gradient = jnp.where(matched, gradient - 1.0, gradient)
        product = small
        while product.shape[0] > 8:
            half = product.shape[0] // 2
            left, right = product[:half], product[half:]
            product = left + right + left * right
        totals[0] += jnp.log1p(product)
        totals[1] += by_eight(jnp.maximum(signed, 0.0))
        totals[2] += by_eight(gradient * scores)
        totals[3] += by_eight(gradient)
        weights[t] = gradient.astype(jnp.bfloat16)
    sums[0] = totals[0] + LN2 * totals[1]
    sums[1] = totals[2]
    sums[2] = totals[3]


def pair_weights(scalars, images, texts, tiles, diagonal=None):
    vmem = pl.BlockSpec(memory_space=pltpu.VMEM)
    n = len(tiles)
    return pl.pallas_call(
        functools.partial(pair_kernel, len(images), len(texts), tiles, diagonal),
        in_specs=[pl.BlockSpec(memory_space=pltpu.SMEM)] + [vmem] * (len(images) + len(texts)),
        out_specs=[vmem, vmem],
        out_shape=[
            jax.ShapeDtypeStruct((n, TILE, TILE), jnp.bfloat16),
            jax.ShapeDtypeStruct((3, 8, TILE), jnp.float32),
        ],
        compiler_params=pltpu.CompilerParams(vmem_limit_bytes=24 * 1024 * 1024),
        cost_estimate=pl.CostEstimate(
            flops=2 * n * TILE * TILE * 1152, bytes_accessed=n << 18, transcendentals=2 * n * TILE * TILE
        ),
    )(scalars, *images, *texts)


def direction_kernel(n_images, n_texts, n_weights, image_out, text_out, where, *refs):
    images, texts = refs[:n_images], refs[n_images : n_images + n_texts]
    weights = refs[n_images + n_texts : n_images + n_texts + n_weights]
    outs = refs[n_images + n_texts + n_weights :]
    for o, i in enumerate(image_out):
        total = None
        for j in range(n_texts):
            a, t = where[i, j]
            term = lax.dot_general(
                weights[a][t], texts[j][...], (((1,), (0,)), ((), ())), preferred_element_type=jnp.float32
            )
            total = term if total is None else total + term
        outs[o][...] = SCALE * total
    for o, j in enumerate(text_out):
        total = None
        for i in range(n_images):
            a, t = where[i, j]
            term = lax.dot_general(
                weights[a][t], images[i][...], (((0,), (0,)), ((), ())), preferred_element_type=jnp.float32
            )
            total = term if total is None else total + term
        outs[len(image_out) + o][...] = SCALE * total


def directions(images, texts, weights, where, image_out, text_out):
    vmem = pl.BlockSpec(memory_space=pltpu.VMEM)
    n_out = len(image_out) + len(text_out)
    n_dots = len(image_out) * len(texts) + len(text_out) * len(images)
    return pl.pallas_call(
        functools.partial(
            direction_kernel, len(images), len(texts), len(weights), tuple(image_out), tuple(text_out), where
        ),
        in_specs=[vmem] * (len(images) + len(texts) + len(weights)),
        out_specs=[vmem] * n_out,
        out_shape=[jax.ShapeDtypeStruct((TILE, 1152), jnp.float32)] * n_out,
        compiler_params=pltpu.CompilerParams(vmem_limit_bytes=24 * 1024 * 1024),
        cost_estimate=pl.CostEstimate(
            flops=2 * n_dots * TILE * TILE * 1152, bytes_accessed=n_dots << 18, transcendentals=0
        ),
    )(*images, *texts, *weights)


def narrow(value):
    return value.astype(jnp.float16)


def wide(value):
    return value.astype(jnp.float32)


def per_device(picture_embedding, caption_embedding, logarithmic_scale_factor, offset_shift):
    rows = picture_embedding.shape[0]
    example_number = rows * 128
    image32, image_inverse = normalize(picture_embedding)
    text32, text_inverse = normalize(caption_embedding)
    image = image32.astype(jnp.bfloat16)
    text = text32.astype(jnp.bfloat16)
    temperature = jnp.exp(logarithmic_scale_factor[0])
    scalars = jnp.stack([temperature, offset_shift[0]])

    image, text = fence(image, text)
    image_z, text_z = fence(send(image, Z, EVEN), send(text, Z, ODD))
    i_own = jnp.concatenate([image, image_z], axis=0)
    t_own = jnp.concatenate([text, text_z], axis=0)

    i_low, i_high, t_low, t_high, s_own = fence(
        send(i_own, "x", UP),
        send(i_own, "x", DOWN),
        send(t_own, "y", UP),
        send(t_own, "y", DOWN),
        send(t_own, "c", SWAP),
    )

    far = [
        send(i_low[:rows], "x", UP),
        send(i_high[rows:], "x", DOWN),
        send(t_low[:rows], "y", UP),
        send(t_high[rows:], "y", DOWN),
    ]
    s_near = send(jnp.concatenate([t_low, t_high], axis=0), "c", SWAP)
    near_images = [i_own, i_low, i_high]
    near_texts = [t_own, t_low, t_high, s_own]
    tiles_a = [(i, j) for j in range(4) for i in range(3)]
    weights_a, sums_a = pair_weights(scalars, near_images, near_texts, tiles_a, 0)
    weights_a, s_near = fence(weights_a, s_near)
    s_low, s_high = s_near[: 2 * rows], s_near[2 * rows :]
    tiles_b = [(i, j) for j in range(2) for i in range(3)]
    weights_b, sums_b = pair_weights(scalars, near_images, [s_low, s_high], tiles_b)
    *far, weights_a, weights_b = fence(*far, weights_a, weights_b)
    i_far = jnp.concatenate(far[:2], axis=0)
    t_far = jnp.concatenate(far[2:], axis=0)
    s_far = send(t_far, "c", SWAP)

    images = [i_own, i_low, i_high, i_far]
    texts = [t_own, t_low, t_high, s_own, s_low, s_high, t_far]
    tiles_c = [(3, j) for j in range(7)] + [(i, 6) for i in range(3)]
    weights_c, sums_c = pair_weights(scalars, images, texts, tiles_c)
    weights_c, s_far = fence(weights_c, s_far)
    tiles_d = [(i, 0) for i in range(4)]
    weights_d, sums_d = pair_weights(scalars, images, [s_far], tiles_d)
    texts = texts + [s_far]
    where = {p: (0, t) for t, p in enumerate(tiles_a)}
    where |= {(i, j + 4): (1, t) for t, (i, j) in enumerate(tiles_b)}
    where |= {p: (2, t) for t, p in enumerate(tiles_c)}
    where |= {(i, 7): (3, t) for t, (i, _) in enumerate(tiles_d)}
    weights = [weights_a, weights_b, weights_c, weights_d]

    value = jnp.sum(sums_a + sums_b + sums_c + sums_d, axis=(1, 2)).reshape(1, 3)
    (ps_far,) = directions(images, texts, weights, where, [], [7])
    *weights, ps_far = fence(*weights, ps_far)
    ps_back = send(narrow(ps_far), "c", SWAP)
    (pi_far,) = directions(images, texts, weights, where, [3], [])
    *weights, pi_far = fence(*weights, pi_far)
    back_x = [send(narrow(pi_far[:rows]), "x", DOWN), send(narrow(pi_far[rows:]), "x", UP)]
    (pt_far,) = directions(images, texts, weights, where, [], [6])
    *weights, pt_far, ps_back = fence(*weights, pt_far, ps_back)
    pt_far = pt_far + wide(ps_back)
    back_y = [send(narrow(pt_far[:rows]), "y", DOWN), send(narrow(pt_far[rows:]), "y", UP)]

    ps_low, ps_high = directions(images, texts, weights, where, [], [4, 5])
    *weights, ps_low, ps_high = fence(*weights, ps_low, ps_high)
    ps_near = send(narrow(jnp.concatenate([ps_low, ps_high], axis=0)), "c", SWAP)
    pi_low, pi_high, pt_low, pt_high = directions(images, texts, weights, where, [1, 2], [1, 2])
    *weights, pt_low, pt_high, ps_near, value = fence(*weights, pt_low, pt_high, ps_near, value)
    pt_low = pt_low + wide(ps_near[: 2 * rows])
    pt_high = pt_high + wide(ps_near[2 * rows :])
    value = value + send(value, "c", SWAP)
    (ps_own,) = directions(images, texts, weights, where, [], [3])
    b0, b1, b2, b3, pi_low, pi_high, pt_low, pt_high, ps_own, value, *weights = fence(
        *back_x, *back_y, pi_low, pi_high, pt_low, pt_high, ps_own, value, *weights
    )
    back = [b0, b1, b2, b3]

    pi_low = jnp.concatenate([pi_low[:rows] + wide(back[0]), pi_low[rows:]], axis=0)
    pi_high = jnp.concatenate([pi_high[:rows], pi_high[rows:] + wide(back[1])], axis=0)
    pt_low = jnp.concatenate([pt_low[:rows] + wide(back[2]), pt_low[rows:]], axis=0)
    pt_high = jnp.concatenate([pt_high[:rows], pt_high[rows:] + wide(back[3])], axis=0)
    near = [
        send(narrow(pi_low), "x", DOWN),
        send(narrow(pi_high), "x", UP),
        send(narrow(pt_low), "y", DOWN),
        send(narrow(pt_high), "y", UP),
    ]
    ps_own = send(narrow(ps_own), "c", SWAP)
    pi_own, pt_own = directions(images, texts, weights, where, [0], [0])
    pi_own, pt_own, ps_own, value = fence(pi_own, pt_own, ps_own, value)
    pt_own = pt_own + wide(ps_own)
    for axis, pairs in ((Z, EVEN), (Z, ODD), ("x", EVEN)):
        value = value + send(value, axis, pairs)
    *near, pi_own, pt_own, value = fence(*near, pi_own, pt_own, value)
    pi_own = pi_own + wide(near[0]) + wide(near[1])
    pt_own = pt_own + wide(near[2]) + wide(near[3])

    last = [send(narrow(pi_own[rows:]), Z, EVEN), send(narrow(pt_own[rows:]), Z, ODD)]
    for axis, pairs in (("x", ODD), ("y", EVEN), ("y", ODD)):
        value = value + send(value, axis, pairs)
    objective_results = value[0] * jnp.stack([jnp.float32(1.0), temperature, jnp.float32(1.0)]) / example_number
    scale = temperature / SCALE
    image_gradient = projection(scale * (pi_own[:rows] + wide(last[0])), image32, image_inverse)
    text_grad = projection(scale * (pt_own[:rows] + wide(last[1])), text32, text_inverse)
    return (image_gradient, text_grad, objective_results)


def solution(mesh):
    mesh = Mesh(mesh.devices.reshape(4, 4, 2, 2, 2), AXES)
    return jax.shard_map(
        per_device,
        mesh=mesh,
        in_specs=(P(AXES, None), P(AXES, None), P(), P()),
        out_specs=(P(AXES, None), P(AXES, None), P()),
        check_vma=False,
    )
```

```python
import functools

import jax
import jax.numpy as jnp
from jax import lax
from jax.experimental import pallas as pl
from jax.experimental.pallas import tpu as pltpu
from jax.sharding import Mesh, PartitionSpec as P

EPS = 1e-06
AXES = ("y", "x", "zh", "zl", "c")
Z = ("zh", "zl")
EVEN = [(0, 1), (1, 0), (2, 3), (3, 2)]
ODD = [(1, 2), (2, 1), (3, 0), (0, 3)]
UP = [(i, (i + 1) % 4) for i in range(4)]
DOWN = [(i, (i - 1) % 4) for i in range(4)]
SWAP = [(0, 1), (1, 0)]
SCALE = 4.0
TILE = 256
LOG2E = 1.4426950408889634
LN2 = 0.6931471805599453


def send(value, axis, pairs):
    return lax.ppermute(value, axis, pairs)


def fence(*values):
    return lax.optimization_barrier(values)


def normalize(embedding):
    widened = embedding.astype(jnp.float32)
    inverse = lax.rsqrt(jnp.sum(widened * widened, axis=1, keepdims=True) + EPS)
    return (widened * inverse, inverse)


def projection(total, unit_rows, inverse):
    radial = jnp.sum(total * unit_rows, axis=1, keepdims=True)
    return (total - radial * unit_rows) * inverse


def by_eight(value):
    return jnp.sum(value.reshape(value.shape[0] // 8, 8, value.shape[1]), axis=0)


def pair_kernel(n_images, n_texts, tiles, diagonal, scalars, *refs):
    images, texts = refs[:n_images], refs[n_images : n_images + n_texts]
    weights, sums = refs[n_images + n_texts :]
    factor = scalars[0] * LOG2E
    offset = scalars[1] * LOG2E
    totals = [jnp.zeros((8, TILE), jnp.float32) for _ in range(4)]
    for t, (i, j) in enumerate(tiles):
        scores = lax.dot_general(
            images[i][...], texts[j][...], (((1,), (1,)), ((), ())), preferred_element_type=jnp.float32
        )
        logits = scores * factor + offset
        small = jnp.exp2(-jnp.abs(logits))
        inverse = pltpu.reciprocal(1.0 + small, approx=True)
        gradient = jnp.where(logits >= 0.0, 1.0, small) * inverse
        signed = logits
        if t == diagonal:
            row = lax.broadcasted_iota(jnp.int32, (TILE, TILE), 0)
            column = lax.broadcasted_iota(jnp.int32, (TILE, TILE), 1)
            matched = (row == column) & (row < TILE // 2)
            signed = jnp.where(matched, -logits, logits)
            gradient = jnp.where(matched, gradient - 1.0, gradient)
        product = small
        while product.shape[0] > 8:
            half = product.shape[0] // 2
            left, right = product[:half], product[half:]
            product = left + right + left * right
        totals[0] += jnp.log1p(product)
        totals[1] += by_eight(jnp.maximum(signed, 0.0))
        totals[2] += by_eight(gradient * scores)
        totals[3] += by_eight(gradient)
        weights[t] = gradient.astype(jnp.bfloat16)
    sums[0] = totals[0] + LN2 * totals[1]
    sums[1] = totals[2]
    sums[2] = totals[3]


def pair_weights(scalars, images, texts, tiles, diagonal=None):
    vmem = pl.BlockSpec(memory_space=pltpu.VMEM)
    n = len(tiles)
    return pl.pallas_call(
        functools.partial(pair_kernel, len(images), len(texts), tiles, diagonal),
        in_specs=[pl.BlockSpec(memory_space=pltpu.SMEM)] + [vmem] * (len(images) + len(texts)),
        out_specs=[vmem, vmem],
        out_shape=[
            jax.ShapeDtypeStruct((n, TILE, TILE), jnp.bfloat16),
            jax.ShapeDtypeStruct((3, 8, TILE), jnp.float32),
        ],
        compiler_params=pltpu.CompilerParams(vmem_limit_bytes=24 * 1024 * 1024),
        cost_estimate=pl.CostEstimate(flops=1, bytes_accessed=1, transcendentals=0),
    )(scalars, *images, *texts)


def stacked_kernel(n_images, n_weights, text_out, where, *refs):
    images, weights = refs[:n_images], refs[n_images : n_images + n_weights]
    before, out = refs[n_images + n_weights : -1], refs[-1]
    for o, j in enumerate(text_out):
        rows = pl.ds(o * TILE, TILE)
        total = before[0][rows, :] if before else None
        for i in range(n_images):
            a, t = where[i, j]
            term = SCALE * lax.dot_general(
                weights[a][t], images[i][...], (((0,), (0,)), ((), ())), preferred_element_type=jnp.float32
            )
            total = term if total is None else total + term
        out[rows, :] = total


def stacked(images, weights, where, text_out, *before):
    vmem = pl.BlockSpec(memory_space=pltpu.VMEM)
    n_out = len(text_out)
    return pl.pallas_call(
        functools.partial(stacked_kernel, len(images), len(weights), tuple(text_out), where),
        in_specs=[vmem] * (len(images) + len(weights) + len(before)),
        out_specs=vmem,
        out_shape=jax.ShapeDtypeStruct((n_out * TILE, 1152), jnp.float32),
        compiler_params=pltpu.CompilerParams(vmem_limit_bytes=24 * 1024 * 1024),
        cost_estimate=pl.CostEstimate(flops=1, bytes_accessed=1, transcendentals=0),
    )(*images, *weights, *before)


def direction_kernel(n_images, n_texts, n_weights, image_out, text_out, where, *refs):
    images, texts = refs[:n_images], refs[n_images : n_images + n_texts]
    weights = refs[n_images + n_texts : n_images + n_texts + n_weights]
    outs = refs[n_images + n_texts + n_weights :]
    for o, i in enumerate(image_out):
        total = None
        for j in range(n_texts):
            a, t = where[i, j]
            term = lax.dot_general(
                weights[a][t], texts[j][...], (((1,), (0,)), ((), ())), preferred_element_type=jnp.float32
            )
            total = term if total is None else total + term
        outs[o][...] = SCALE * total
    for o, j in enumerate(text_out):
        total = None
        for i in range(n_images):
            a, t = where[i, j]
            term = lax.dot_general(
                weights[a][t], images[i][...], (((0,), (0,)), ((), ())), preferred_element_type=jnp.float32
            )
            total = term if total is None else total + term
        outs[len(image_out) + o][...] = SCALE * total


def directions(images, texts, weights, where, image_out, text_out):
    vmem = pl.BlockSpec(memory_space=pltpu.VMEM)
    n_out = len(image_out) + len(text_out)
    n_dots = len(image_out) * len(texts) + len(text_out) * len(images)
    return pl.pallas_call(
        functools.partial(
            direction_kernel, len(images), len(texts), len(weights), tuple(image_out), tuple(text_out), where
        ),
        in_specs=[vmem] * (len(images) + len(texts) + len(weights)),
        out_specs=[vmem] * n_out,
        out_shape=[jax.ShapeDtypeStruct((TILE, 1152), jnp.float32)] * n_out,
        compiler_params=pltpu.CompilerParams(vmem_limit_bytes=24 * 1024 * 1024),
        cost_estimate=pl.CostEstimate(flops=1, bytes_accessed=1, transcendentals=0),
    )(*images, *texts, *weights)


def narrow(value):
    return value.astype(jnp.float16)


def wide(value):
    return value.astype(jnp.float32)


def per_device(picture_embedding, caption_embedding, logarithmic_scale_factor, offset_shift):
    rows = picture_embedding.shape[0]
    example_number = rows * 128
    (both,) = fence(jnp.concatenate([picture_embedding, caption_embedding], axis=0))
    unit32, inverse = normalize(both)
    unit = unit32.astype(jnp.bfloat16)
    image, text = unit[:rows], unit[rows:]
    temperature = jnp.exp(logarithmic_scale_factor[0])
    scalars = jnp.stack([temperature, offset_shift[0]])

    image_z, text_z = fence(send(image, Z, EVEN), send(text, Z, ODD))
    i_own = jnp.concatenate([image, image_z], axis=0)
    t_own = jnp.concatenate([text, text_z], axis=0)

    scalars, i_low, i_high, t_low, t_high, text_s, text_zs = fence(
        scalars,
        send(i_own, "x", UP),
        send(i_own, "x", DOWN),
        send(t_own, "y", UP),
        send(t_own, "y", DOWN),
        send(text, "c", SWAP),
        send(text_z, "c", SWAP),
    )
    s_own = jnp.concatenate([text_s, text_zs], axis=0)

    far = [
        send(i_low[:rows], "x", UP),
        send(i_high[rows:], "x", DOWN),
        send(t_low[:rows], "y", UP),
        send(t_high[rows:], "y", DOWN),
    ]
    s_near = send(jnp.concatenate([t_low, t_high], axis=0), "c", SWAP)
    near_images = [i_own, i_low, i_high]
    near_texts = [t_own, t_low, t_high, s_own]
    tiles_a = [(i, j) for j in range(4) for i in range(3)]
    weights_a, sums_a = pair_weights(scalars, near_images, near_texts, tiles_a, 0)
    weights_a, s_near = fence(weights_a, s_near)
    s_low, s_high = s_near[: 2 * rows], s_near[2 * rows :]
    tiles_b = [(i, j) for j in range(2) for i in range(3)]
    weights_b, sums_b = pair_weights(scalars, near_images, [s_low, s_high], tiles_b)
    where = {p: (0, t) for t, p in enumerate(tiles_a)}
    where |= {(i, j + 4): (1, t) for t, (i, j) in enumerate(tiles_b)}
    ps_near = stacked(near_images, [weights_a, weights_b], where, [4, 5, 3])
    *far, weights_a, weights_b, ps_near = fence(*far, weights_a, weights_b, ps_near)
    i_far = jnp.concatenate(far[:2], axis=0)
    t_far = jnp.concatenate(far[2:], axis=0)
    s_far = send(t_far, "c", SWAP)

    images = [i_own, i_low, i_high, i_far]
    texts = [t_own, t_low, t_high, s_own, s_low, s_high, t_far]
    tiles_c = [(3, j) for j in range(7)] + [(i, 6) for i in range(3)]
    weights_c, sums_c = pair_weights(scalars, images, texts, tiles_c)
    weights_c, s_far = fence(weights_c, s_far)
    tiles_d = [(i, 0) for i in range(4)]
    weights_d, sums_d = pair_weights(scalars, images, [s_far], tiles_d)
    texts = texts + [s_far]
    where |= {p: (2, t) for t, p in enumerate(tiles_c)}
    where |= {(i, 7): (3, t) for t, (i, _) in enumerate(tiles_d)}
    weights = [weights_a, weights_b, weights_c, weights_d]

    (ps_far,) = directions(images, texts, weights, where, [], [7])
    *weights, ps_far = fence(*weights, narrow(ps_far))
    ps_far = send(ps_far, "c", SWAP)
    value = jnp.sum(sums_a + sums_b + sums_c + sums_d, axis=(1, 2)).reshape(1, 3)
    pi_far, pt_far = directions(images, texts, weights, where, [3], [6])
    from_far = {(0, j): where[3, j] for j in (4, 5, 3)}
    ps_near = narrow(stacked([i_far], weights, from_far, [4, 5, 3], ps_near))
    pi_far = narrow(pi_far)
    pt_far = narrow(pt_far + wide(ps_far))
    pi_far, pt_far, ps_near, value, *weights = fence(pi_far, pt_far, ps_near, value, *weights)
    back = [
        send(pi_far[:rows], "x", DOWN),
        send(pi_far[rows:], "x", UP),
        send(pt_far[:rows], "y", DOWN),
        send(pt_far[rows:], "y", UP),
    ]
    ps_near = send(ps_near, "c", SWAP)
    pi_low, pi_high, pi_own, pt_low, pt_high, pt_own = directions(images, texts, weights, where, [1, 2, 0], [1, 2, 0])
    *back, ps_near, pi_low, pi_high, pi_own, pt_low, pt_high, pt_own = fence(
        *back, ps_near, pi_low, pi_high, pi_own, pt_low, pt_high, pt_own
    )

    first, second = ((0, rows), (0, 0)), ((rows, 0), (0, 0))
    near = [
        narrow(pi_low + jnp.pad(wide(back[0]), first)),
        narrow(pi_high + jnp.pad(wide(back[1]), second)),
        narrow(pt_low + wide(ps_near[: 2 * rows]) + jnp.pad(wide(back[2]), first)),
        narrow(pt_high + wide(ps_near[2 * rows : 4 * rows]) + jnp.pad(wide(back[3]), second)),
    ]
    *near, value = fence(*near, value)
    near = [
        send(near[0], "x", DOWN),
        send(near[1], "x", UP),
        send(near[2], "y", DOWN),
        send(near[3], "y", UP),
    ]
    for axis, pairs in (("c", SWAP), (Z, EVEN), (Z, ODD), ("x", EVEN)):
        value = value + send(value, axis, pairs)
    pt_own = pt_own + wide(ps_near[4 * rows :])
    *near, pi_own, pt_own, value = fence(*near, pi_own, pt_own, value)
    pi_own = pi_own + wide(near[0]) + wide(near[1])
    pt_own = pt_own + wide(near[2]) + wide(near[3])

    last = [narrow(pi_own[rows:]), narrow(pt_own[rows:])]
    *last, value = fence(*last, value)
    last = [send(last[0], Z, EVEN), send(last[1], Z, ODD)]
    for axis, pairs in (("x", ODD), ("y", EVEN), ("y", ODD)):
        value = value + send(value, axis, pairs)
    objective_results = value[0] * jnp.stack([jnp.float32(1.0), temperature, jnp.float32(1.0)]) / example_number
    scale = temperature / SCALE
    image_gradient = projection(scale * (pi_own[:rows] + wide(last[0])), unit32[:rows], inverse[:rows])
    text_grad = projection(scale * (pt_own[:rows] + wide(last[1])), unit32[rows:], inverse[rows:])
    return (image_gradient, text_grad, objective_results)


def solution(mesh):
    mesh = Mesh(mesh.devices.reshape(4, 4, 2, 2, 2), AXES)
    return jax.shard_map(
        per_device,
        mesh=mesh,
        in_specs=(P(AXES, None), P(AXES, None), P(), P()),
        out_specs=(P(AXES, None), P(AXES, None), P()),
        check_vma=False,
    )
```

```python
import functools

import jax
import jax.numpy as jnp
from jax import lax
from jax.experimental import pallas as pl
from jax.experimental.pallas import tpu as pltpu
from jax.sharding import Mesh, PartitionSpec as P

EPS = 1e-06
AXES = ("y", "x", "zh", "zl", "c")
Z = ("zh", "zl")
EVEN = [(0, 1), (1, 0), (2, 3), (3, 2)]
ODD = [(1, 2), (2, 1), (3, 0), (0, 3)]
UP = [(i, (i + 1) % 4) for i in range(4)]
DOWN = [(i, (i - 1) % 4) for i in range(4)]
SWAP = [(0, 1), (1, 0)]
SCALE = 4.0
TILE = 256
LOG2E = 1.4426950408889634
LN2 = 0.6931471805599453


def send(value, axis, pairs):
    return lax.ppermute(value, axis, pairs)


def fence(*values):
    return lax.optimization_barrier(values)


def normalize(embedding):
    widened = embedding.astype(jnp.float32)
    inverse = lax.rsqrt(jnp.sum(widened * widened, axis=1, keepdims=True) + EPS)
    return (widened * inverse, inverse)


def projection(total, unit_rows, inverse):
    radial = jnp.sum(total * unit_rows, axis=1, keepdims=True)
    return (total - radial * unit_rows) * inverse


def by_eight(value):
    return jnp.sum(value.reshape(value.shape[0] // 8, 8, value.shape[1]), axis=0)


def pair_tile(scores, factor, offset, diagonal, totals):
    logits = scores * factor + offset
    small = jnp.exp2(-jnp.abs(logits))
    inverse = pltpu.reciprocal(1.0 + small, approx=True)
    gradient = jnp.where(logits >= 0.0, 1.0, small) * inverse
    signed = logits
    if diagonal:
        row = lax.broadcasted_iota(jnp.int32, (TILE, TILE), 0)
        column = lax.broadcasted_iota(jnp.int32, (TILE, TILE), 1)
        matched = (row == column) & (row < TILE // 2)
        signed = jnp.where(matched, -logits, logits)
        gradient = jnp.where(matched, gradient - 1.0, gradient)
    product = small
    while product.shape[0] > 8:
        half = product.shape[0] // 2
        left, right = product[:half], product[half:]
        product = left + right + left * right
    totals[0] += jnp.log1p(product)
    totals[1] += by_eight(jnp.maximum(signed, 0.0))
    totals[2] += by_eight(gradient * scores)
    totals[3] += by_eight(gradient)
    return gradient.astype(jnp.bfloat16)


def block_kernel(n_images, n_texts, n_old, n_before, tiles, diagonal, where, jobs, *refs):
    refs = list(refs)
    take = lambda n: [refs.pop(0) for _ in range(n)]
    scalars = take(1)[0] if tiles else None
    images, texts, old, before = take(n_images), take(n_texts), take(n_old), take(n_before)
    if tiles:
        new, sums = take(2)
        factor = scalars[0] * LOG2E
        offset = scalars[1] * LOG2E
        totals = [jnp.zeros((8, TILE), jnp.float32) for _ in range(4)]
        for t, (i, j) in enumerate(tiles):
            scores = lax.dot_general(
                images[i][...], texts[j][...], (((1,), (1,)), ((), ())), preferred_element_type=jnp.float32
            )
            new[t] = pair_tile(scores, factor, offset, t == diagonal, totals)
        sums[0] = totals[0] + LN2 * totals[1]
        sums[1] = totals[2]
        sums[2] = totals[3]
        old = old + [new]
    for out, row, kind, index, over, base in jobs:
        total = None
        for k in over:
            a, t = where[(index, k) if kind == "image" else (k, index)]
            rows, contract = (texts[k], 1) if kind == "image" else (images[k], 0)
            term = lax.dot_general(
                old[a][t], rows[...], (((contract,), (0,)), ((), ())), preferred_element_type=jnp.float32
            )
            total = term if total is None else total + term
        total = SCALE * total
        place = pl.ds(row * TILE, TILE)
        refs[out][place, :] = total if base is None else total + before[base][place, :]


def block(scalars, images, texts, old, where, tiles=(), diagonal=None, jobs=(), outs=(), before=()):
    vmem = pl.BlockSpec(memory_space=pltpu.VMEM)
    head = [scalars] if tiles else []
    out_shape = [jax.ShapeDtypeStruct((n * TILE, 1152), jnp.float32) for n in outs]
    if tiles:
        out_shape = [
            jax.ShapeDtypeStruct((len(tiles), TILE, TILE), jnp.bfloat16),
            jax.ShapeDtypeStruct((3, 8, TILE), jnp.float32),
        ] + out_shape
    return pl.pallas_call(
        functools.partial(
            block_kernel,
            len(images),
            len(texts),
            len(old),
            len(before),
            tuple(tiles),
            diagonal,
            dict(where),
            tuple(jobs),
        ),
        in_specs=[pl.BlockSpec(memory_space=pltpu.SMEM)] * len(head)
        + [vmem] * (len(images) + len(texts) + len(old) + len(before)),
        out_specs=[vmem] * len(out_shape),
        out_shape=out_shape,
        compiler_params=pltpu.CompilerParams(vmem_limit_bytes=24 * 1024 * 1024),
        cost_estimate=pl.CostEstimate(flops=1, bytes_accessed=1, transcendentals=0),
    )(*head, *images, *texts, *old, *before)


def narrow(value):
    return value.astype(jnp.float16)


def wide(value):
    return value.astype(jnp.float32)


def per_device(picture_embedding, caption_embedding, logarithmic_scale_factor, offset_shift):
    rows = picture_embedding.shape[0]
    example_number = rows * 128
    (both,) = fence(jnp.concatenate([picture_embedding, caption_embedding], axis=0))
    unit32, inverse = normalize(both)
    unit = unit32.astype(jnp.bfloat16)
    image, text = unit[:rows], unit[rows:]
    temperature = jnp.exp(logarithmic_scale_factor[0])
    scalars = jnp.stack([temperature, offset_shift[0]])

    image_z, text_z = fence(send(image, Z, EVEN), send(text, Z, ODD))
    i_own = jnp.concatenate([image, image_z], axis=0)
    t_own = jnp.concatenate([text, text_z], axis=0)

    scalars, i_low, i_high, t_low, t_high, text_s, text_zs = fence(
        scalars,
        send(i_own, "x", UP),
        send(i_own, "x", DOWN),
        send(t_own, "y", UP),
        send(t_own, "y", DOWN),
        send(text, "c", SWAP),
        send(text_z, "c", SWAP),
    )
    s_own = jnp.concatenate([text_s, text_zs], axis=0)

    far = [
        send(i_low[:rows], "x", UP),
        send(i_high[rows:], "x", DOWN),
        send(t_low[:rows], "y", UP),
        send(t_high[rows:], "y", DOWN),
    ]
    s_near = send(jnp.concatenate([t_low, t_high], axis=0), "c", SWAP)
    near_images = [i_own, i_low, i_high]
    near_texts = [t_own, t_low, t_high, s_own]
    where = {}

    def place(number, tiles):
        where.update({p: (number, t) for t, p in enumerate(tiles)})
        return tiles

    tiles_a = place(0, [(i, j) for j in range(4) for i in range(3)])
    weights_a, sums_a = block(scalars, near_images, near_texts, [], where, tiles_a, 0)
    weights_a, s_near = fence(weights_a, s_near)
    s_low, s_high = s_near[: 2 * rows], s_near[2 * rows :]
    near_texts = [t_own, t_low, t_high, s_own, s_low, s_high]
    tiles_b = place(1, [(i, j) for j in (4, 5) for i in range(3)])
    shared = [(0, n, "text", j, (0, 1, 2), None) for n, j in enumerate((4, 5, 3))]
    weights_b, sums_b, ps_near = block(
        scalars, near_images, near_texts, [weights_a], where, tiles_b, None, shared, [3]
    )
    *far, weights_a, weights_b, ps_near = fence(*far, weights_a, weights_b, ps_near)
    i_far = jnp.concatenate(far[:2], axis=0)
    t_far = jnp.concatenate(far[2:], axis=0)
    s_far = send(t_far, "c", SWAP)

    images = [i_own, i_low, i_high, i_far]
    texts = [t_own, t_low, t_high, s_own, s_low, s_high, t_far]
    weights = [weights_a, weights_b]
    tiles_c = place(2, [(3, j) for j in range(7)] + [(i, 6) for i in range(3)])
    weights_c, sums_c, pi_far, pt_far = block(
        scalars,
        images,
        texts,
        weights,
        where,
        tiles_c,
        None,
        [(0, 0, "image", 3, tuple(range(7)), None), (1, 0, "text", 6, (0, 1, 2, 3), None)],
        [1, 1],
    )
    weights_c, s_far = fence(weights_c, s_far)
    texts = texts + [s_far]
    tiles_d = place(3, [(i, 7) for i in range(4)])
    weights_d, sums_d, ps_far = block(
        scalars, images, texts, weights + [weights_c], where, tiles_d, None, [(0, 0, "text", 7, (0, 1, 2, 3), None)], [1]
    )
    weights = [weights_a, weights_b, weights_c, weights_d]

    *weights, ps_far = fence(*weights, narrow(ps_far))
    ps_far = send(ps_far, "c", SWAP)
    value = jnp.sum(sums_a + sums_b + sums_c + sums_d, axis=(1, 2)).reshape(1, 3)
    pi_far, ps_near = block(
        None,
        images,
        texts,
        weights,
        where,
        jobs=[(0, 0, "image", 3, (7,), 0)] + [(1, n, "text", j, (3,), 1) for n, j in enumerate((4, 5, 3))],
        outs=[1, 3],
        before=[pi_far, ps_near],
    )
    ps_near = narrow(ps_near)
    pi_far = narrow(pi_far)
    pt_far = narrow(pt_far + wide(ps_far))
    pi_far, pt_far, ps_near, value, *weights = fence(pi_far, pt_far, ps_near, value, *weights)
    back = [
        send(pi_far[:rows], "x", DOWN),
        send(pi_far[rows:], "x", UP),
        send(pt_far[:rows], "y", DOWN),
        send(pt_far[rows:], "y", UP),
    ]
    ps_near = send(ps_near, "c", SWAP)
    pi_low, pi_high, pi_own, pt_low, pt_high, pt_own = block(
        None,
        images,
        texts,
        weights,
        where,
        jobs=[(n, 0, "image", i, tuple(range(8)), None) for n, i in enumerate((1, 2, 0))]
        + [(n + 3, 0, "text", j, (0, 1, 2, 3), None) for n, j in enumerate((1, 2, 0))],
        outs=[1] * 6,
    )
    *back, ps_near, pi_low, pi_high, pi_own, pt_low, pt_high, pt_own = fence(
        *back, ps_near, pi_low, pi_high, pi_own, pt_low, pt_high, pt_own
    )

    first, second = ((0, rows), (0, 0)), ((rows, 0), (0, 0))
    near = [
        narrow(pi_low + jnp.pad(wide(back[0]), first)),
        narrow(pi_high + jnp.pad(wide(back[1]), second)),
        narrow(pt_low + wide(ps_near[: 2 * rows]) + jnp.pad(wide(back[2]), first)),
        narrow(pt_high + wide(ps_near[2 * rows : 4 * rows]) + jnp.pad(wide(back[3]), second)),
    ]
    *near, value = fence(*near, value)
    near = [
        send(near[0], "x", DOWN),
        send(near[1], "x", UP),
        send(near[2], "y", DOWN),
        send(near[3], "y", UP),
    ]
    for axis, pairs in (("c", SWAP), (Z, EVEN), (Z, ODD), ("x", EVEN)):
        value = value + send(value, axis, pairs)
    pt_own = pt_own + wide(ps_near[4 * rows :])
    *near, pi_own, pt_own, value = fence(*near, pi_own, pt_own, value)
    pi_own = pi_own + wide(near[0]) + wide(near[1])
    pt_own = pt_own + wide(near[2]) + wide(near[3])

    last = [narrow(pi_own[rows:]), narrow(pt_own[rows:])]
    *last, value = fence(*last, value)
    last = [send(last[0], Z, EVEN), send(last[1], Z, ODD)]
    for axis, pairs in (("x", ODD), ("y", EVEN)):
        value = value + send(value, axis, pairs)
    *last, value = fence(*last, value)
    value = value + send(value, "y", ODD)
    objective_results = value[0] * jnp.stack([jnp.float32(1.0), temperature, jnp.float32(1.0)]) / example_number
    scale = temperature / SCALE
    image_gradient = projection(scale * (pi_own[:rows] + wide(last[0])), unit32[:rows], inverse[:rows])
    text_grad = projection(scale * (pt_own[:rows] + wide(last[1])), unit32[rows:], inverse[rows:])
    return (image_gradient, text_grad, objective_results)


def solution(mesh):
    mesh = Mesh(mesh.devices.reshape(4, 4, 2, 2, 2), AXES)
    return jax.shard_map(
        per_device,
        mesh=mesh,
        in_specs=(P(AXES, None), P(AXES, None), P(), P()),
        out_specs=(P(AXES, None), P(AXES, None), P()),
        check_vma=False,
    )
```

```python
import functools

import jax
import jax.numpy as jnp
from jax import lax
from jax.experimental import pallas as pl
from jax.experimental.pallas import tpu as pltpu
from jax.sharding import Mesh, PartitionSpec as P

EPS = 1e-06
AXES = ("y", "x", "zh", "zl", "c")
Z = ("zh", "zl")
EVEN = [(0, 1), (1, 0), (2, 3), (3, 2)]
ODD = [(1, 2), (2, 1), (3, 0), (0, 3)]
UP = [(i, (i + 1) % 4) for i in range(4)]
DOWN = [(i, (i - 1) % 4) for i in range(4)]
SWAP = [(0, 1), (1, 0)]
SCALE = 4.0
TILE = 256
LOG2E = 1.4426950408889634
LN2 = 0.6931471805599453


def send(value, axis, pairs):
    return lax.ppermute(value, axis, pairs)


def fence(*values):
    return lax.optimization_barrier(values)


def normalize(embedding):
    widened = embedding.astype(jnp.float32)
    inverse = lax.rsqrt(jnp.sum(widened * widened, axis=1, keepdims=True) + EPS)
    return (widened * inverse, inverse)


def projection(total, unit_rows, inverse):
    radial = jnp.sum(total * unit_rows, axis=1, keepdims=True)
    return (total - radial * unit_rows) * inverse


def by_eight(value):
    return jnp.sum(value.reshape(value.shape[0] // 8, 8, value.shape[1]), axis=0)


def pair_tile(scores, factor, offset, diagonal, totals):
    logits = scores * factor + offset
    small = jnp.exp2(-jnp.abs(logits))
    inverse = pltpu.reciprocal(1.0 + small, approx=True)
    gradient = jnp.where(logits >= 0.0, 1.0, small) * inverse
    signed = logits
    if diagonal:
        row = lax.broadcasted_iota(jnp.int32, (TILE, TILE), 0)
        column = lax.broadcasted_iota(jnp.int32, (TILE, TILE), 1)
        matched = (row == column) & (row < TILE // 2)
        signed = jnp.where(matched, -logits, logits)
        gradient = jnp.where(matched, gradient - 1.0, gradient)
    product = small
    while product.shape[0] > 8:
        half = product.shape[0] // 2
        left, right = product[:half], product[half:]
        product = left + right + left * right
    totals[0] += jnp.log1p(product)
    totals[1] += by_eight(jnp.maximum(signed, 0.0))
    totals[2] += by_eight(gradient * scores)
    totals[3] += by_eight(gradient)
    return gradient.astype(jnp.bfloat16)


def block_kernel(n_images, n_texts, n_old, n_before, tiles, diagonal, where, jobs, *refs):
    refs = list(refs)
    take = lambda n: [refs.pop(0) for _ in range(n)]
    scalars = take(1)[0] if tiles else None
    images, texts, old, before = take(n_images), take(n_texts), take(n_old), take(n_before)
    if tiles:
        new, sums = take(2)
        factor = scalars[0] * LOG2E
        offset = scalars[1] * LOG2E
        totals = [jnp.zeros((8, TILE), jnp.float32) for _ in range(4)]
        for t, (i, j) in enumerate(tiles):
            scores = lax.dot_general(
                images[i][...], texts[j][...], (((1,), (1,)), ((), ())), preferred_element_type=jnp.float32
            )
            new[t] = pair_tile(scores, factor, offset, t == diagonal, totals)
        sums[0] = totals[0] + LN2 * totals[1]
        sums[1] = totals[2]
        sums[2] = totals[3]
        old = old + [new]
    for out, row, kind, index, over, base in jobs:
        total = None
        for k in over:
            a, t = where[(index, k) if kind == "image" else (k, index)]
            rows, contract = (texts[k], 1) if kind == "image" else (images[k], 0)
            term = lax.dot_general(
                old[a][t], rows[...], (((contract,), (0,)), ((), ())), preferred_element_type=jnp.float32
            )
            total = term if total is None else total + term
        total = SCALE * total
        place = pl.ds(row * TILE, TILE)
        refs[out][place, :] = total if base is None else total + before[base][place, :]


def block(scalars, images, texts, old, where, tiles=(), diagonal=None, jobs=(), outs=(), before=()):
    vmem = pl.BlockSpec(memory_space=pltpu.VMEM)
    head = [scalars] if tiles else []
    out_shape = [jax.ShapeDtypeStruct((n * TILE, 1152), jnp.float32) for n in outs]
    if tiles:
        out_shape = [
            jax.ShapeDtypeStruct((len(tiles), TILE, TILE), jnp.bfloat16),
            jax.ShapeDtypeStruct((3, 8, TILE), jnp.float32),
        ] + out_shape
    return pl.pallas_call(
        functools.partial(
            block_kernel,
            len(images),
            len(texts),
            len(old),
            len(before),
            tuple(tiles),
            diagonal,
            dict(where),
            tuple(jobs),
        ),
        in_specs=[pl.BlockSpec(memory_space=pltpu.SMEM)] * len(head)
        + [vmem] * (len(images) + len(texts) + len(old) + len(before)),
        out_specs=[vmem] * len(out_shape),
        out_shape=out_shape,
        compiler_params=pltpu.CompilerParams(vmem_limit_bytes=24 * 1024 * 1024),
        cost_estimate=pl.CostEstimate(flops=1, bytes_accessed=1, transcendentals=0),
    )(*head, *images, *texts, *old, *before)


def narrow(value):
    return value.astype(jnp.float16)


def wide(value):
    return value.astype(jnp.float32)


def per_device(picture_embedding, caption_embedding, logarithmic_scale_factor, offset_shift):
    rows = picture_embedding.shape[0]
    example_number = rows * 128
    (both,) = fence(jnp.concatenate([picture_embedding, caption_embedding], axis=0))
    unit32, inverse = normalize(both)
    unit = unit32.astype(jnp.bfloat16)
    image, text = unit[:rows], unit[rows:]
    temperature = jnp.exp(logarithmic_scale_factor[0])
    scalars = jnp.stack([temperature, offset_shift[0]])

    image_z, text_z = fence(send(image, Z, EVEN), send(text, Z, ODD))
    i_own = jnp.concatenate([image, image_z], axis=0)
    t_own = jnp.concatenate([text, text_z], axis=0)

    scalars, i_low, i_high, t_low, t_high, text_s, text_zs = fence(
        scalars,
        send(i_own, "x", UP),
        send(i_own, "x", DOWN),
        send(t_own, "y", UP),
        send(t_own, "y", DOWN),
        send(text, "c", SWAP),
        send(text_z, "c", SWAP),
    )
    s_own = jnp.concatenate([text_s, text_zs], axis=0)

    far = [
        send(i_low[:rows], "x", UP),
        send(i_high[rows:], "x", DOWN),
        send(t_low[:rows], "y", UP),
        send(t_high[rows:], "y", DOWN),
    ]
    s_near = send(jnp.concatenate([t_low, t_high], axis=0), "c", SWAP)
    near_images = [i_own, i_low, i_high]
    near_texts = [t_own, t_low, t_high, s_own]
    where = {}

    def place(number, tiles):
        where.update({p: (number, t) for t, p in enumerate(tiles)})
        return tiles

    tiles_a = place(0, [(i, j) for j in range(4) for i in range(3)])
    weights_a, sums_a = block(scalars, near_images, near_texts, [], where, tiles_a, 0)
    weights_a, s_near = fence(weights_a, s_near)
    s_low, s_high = s_near[: 2 * rows], s_near[2 * rows :]
    near_texts = [t_own, t_low, t_high, s_own, s_low, s_high]
    tiles_b = place(1, [(i, j) for j in (4, 5) for i in range(3)])
    shared = [(0, n, "text", j, (0, 1, 2), None) for n, j in enumerate((4, 5, 3))]
    weights_b, sums_b, ps_near = block(
        scalars, near_images, near_texts, [weights_a], where, tiles_b, None, shared, [3]
    )
    *far, weights_a, weights_b, ps_near = fence(*far, weights_a, weights_b, ps_near)
    i_far = jnp.concatenate(far[:2], axis=0)
    t_far = jnp.concatenate(far[2:], axis=0)
    s_far = send(t_far, "c", SWAP)

    images = [i_own, i_low, i_high, i_far]
    texts = [t_own, t_low, t_high, s_own, s_low, s_high, t_far]
    weights = [weights_a, weights_b]
    tiles_c = place(2, [(3, j) for j in range(7)] + [(i, 6) for i in range(3)])
    weights_c, sums_c, pi_far, pt_far = block(
        scalars,
        images,
        texts,
        weights,
        where,
        tiles_c,
        None,
        [(0, 0, "image", 3, tuple(range(7)), None), (1, 0, "text", 6, (0, 1, 2, 3), None)],
        [1, 1],
    )
    weights_c, s_far = fence(weights_c, s_far)
    texts = texts + [s_far]
    tiles_d = place(3, [(i, 7) for i in range(4)])
    weights_d, sums_d, ps_far = block(
        scalars, images, texts, weights + [weights_c], where, tiles_d, None, [(0, 0, "text", 7, (0, 1, 2, 3), None)], [1]
    )
    weights = [weights_a, weights_b, weights_c, weights_d]

    value = jnp.sum(sums_a + sums_b + sums_c + sums_d, axis=(1, 2)).reshape(1, 3)
    *weights, ps_far, value = fence(*weights, narrow(ps_far), value)
    ps_far = send(ps_far, "c", SWAP)
    value = value + send(value, "c", SWAP)
    pi_far, ps_near = block(
        None,
        images,
        texts,
        weights,
        where,
        jobs=[(0, 0, "image", 3, (7,), 0)] + [(1, n, "text", j, (3,), 1) for n, j in enumerate((4, 5, 3))],
        outs=[1, 3],
        before=[pi_far, ps_near],
    )
    ps_near = narrow(ps_near)
    pi_far = narrow(pi_far)
    pt_far = narrow(pt_far + wide(ps_far))
    pi_far, pt_far, ps_near, value, *weights = fence(pi_far, pt_far, ps_near, value, *weights)
    back = [
        send(pi_far[:rows], "x", DOWN),
        send(pi_far[rows:], "x", UP),
        send(pt_far[:rows], "y", DOWN),
        send(pt_far[rows:], "y", UP),
    ]
    ps_near = send(ps_near, "c", SWAP)
    pi_low, pi_high, pi_own, pt_low, pt_high, pt_own = block(
        None,
        images,
        texts,
        weights,
        where,
        jobs=[(n, 0, "image", i, tuple(range(8)), None) for n, i in enumerate((1, 2, 0))]
        + [(n + 3, 0, "text", j, (0, 1, 2, 3), None) for n, j in enumerate((1, 2, 0))],
        outs=[1] * 6,
    )
    *back, ps_near, pi_low, pi_high, pi_own, pt_low, pt_high, pt_own = fence(
        *back, ps_near, pi_low, pi_high, pi_own, pt_low, pt_high, pt_own
    )

    first, second = ((0, rows), (0, 0)), ((rows, 0), (0, 0))
    near = [
        narrow(pi_low + jnp.pad(wide(back[0]), first)),
        narrow(pi_high + jnp.pad(wide(back[1]), second)),
        narrow(pt_low + wide(ps_near[: 2 * rows]) + jnp.pad(wide(back[2]), first)),
        narrow(pt_high + wide(ps_near[2 * rows : 4 * rows]) + jnp.pad(wide(back[3]), second)),
    ]
    *near, value = fence(*near, value)
    near = [
        send(near[0], "x", DOWN),
        send(near[1], "x", UP),
        send(near[2], "y", DOWN),
        send(near[3], "y", UP),
    ]
    for axis, pairs in ((Z, EVEN), (Z, ODD), ("x", EVEN)):
        value = value + send(value, axis, pairs)
    pt_own = pt_own + wide(ps_near[4 * rows :])
    *near, pi_own, pt_own, value = fence(*near, pi_own, pt_own, value)
    pi_own = pi_own + wide(near[0]) + wide(near[1])
    pt_own = pt_own + wide(near[2]) + wide(near[3])

    last = [narrow(pi_own[rows:]), narrow(pt_own[rows:])]
    *last, value = fence(*last, value)
    last = [send(last[0], Z, EVEN), send(last[1], Z, ODD)]
    value = value + send(value, "x", ODD)
    low, far, high = (send(value, "y", [(i, (i + step) % 4) for i in range(4)]) for step in (1, 2, 3))
    scale = temperature / SCALE
    image_gradient = projection(scale * (pi_own[:rows] + wide(last[0])), unit32[:rows], inverse[:rows])
    text_grad = projection(scale * (pt_own[:rows] + wide(last[1])), unit32[rows:], inverse[rows:])
    image_gradient, text_grad, value, low, far, high = fence(image_gradient, text_grad, value, low, far, high)
    value = (value + far) + (low + high)
    objective_results = value[0] * jnp.stack([jnp.float32(1.0), temperature, jnp.float32(1.0)]) / example_number
    return (image_gradient, text_grad, objective_results)


def solution(mesh):
    mesh = Mesh(mesh.devices.reshape(4, 4, 2, 2, 2), AXES)
    return jax.shard_map(
        per_device,
        mesh=mesh,
        in_specs=(P(AXES, None), P(AXES, None), P(), P()),
        out_specs=(P(AXES, None), P(AXES, None), P()),
        check_vma=False,
    )
```

```python
import functools

import jax
import jax.numpy as jnp
from jax import lax
from jax.experimental import pallas as pl
from jax.experimental.pallas import tpu as pltpu
from jax.sharding import Mesh, PartitionSpec as P

EPS = 1e-06
AXES = ("y", "x", "zh", "zl", "c")
Z = ("zh", "zl")
EVEN = [(0, 1), (1, 0), (2, 3), (3, 2)]
ODD = [(1, 2), (2, 1), (3, 0), (0, 3)]
UP = [(i, (i + 1) % 4) for i in range(4)]
DOWN = [(i, (i - 1) % 4) for i in range(4)]
SWAP = [(0, 1), (1, 0)]
SCALE = 4.0
TILE = 256
LOG2E = 1.4426950408889634
LN2 = 0.6931471805599453


def send(value, axis, pairs):
    return lax.ppermute(value, axis, pairs)


def fence(*values):
    return lax.optimization_barrier(values)


def normalize(embedding):
    widened = embedding.astype(jnp.float32)
    inverse = lax.rsqrt(jnp.sum(widened * widened, axis=1, keepdims=True) + EPS)
    return (widened * inverse, inverse)


def projection(total, unit_rows, inverse):
    radial = jnp.sum(total * unit_rows, axis=1, keepdims=True)
    return (total - radial * unit_rows) * inverse


def by_eight(value):
    return jnp.sum(value.reshape(value.shape[0] // 8, 8, value.shape[1]), axis=0)


def pair_tile(scores, factor, offset, diagonal, totals):
    logits = scores * factor + offset
    small = jnp.exp2(-jnp.abs(logits))
    inverse = pltpu.reciprocal(1.0 + small, approx=True)
    gradient = jnp.where(logits >= 0.0, 1.0, small) * inverse
    signed = logits
    if diagonal:
        row = lax.broadcasted_iota(jnp.int32, (TILE, TILE), 0)
        column = lax.broadcasted_iota(jnp.int32, (TILE, TILE), 1)
        matched = (row == column) & (row < TILE // 2)
        signed = jnp.where(matched, -logits, logits)
        gradient = jnp.where(matched, gradient - 1.0, gradient)
    product = small
    while product.shape[0] > 8:
        half = product.shape[0] // 2
        left, right = product[:half], product[half:]
        product = left + right + left * right
    totals[0] += jnp.log1p(product)
    totals[1] += by_eight(jnp.maximum(signed, 0.0))
    totals[2] += by_eight(gradient * scores)
    totals[3] += by_eight(gradient)
    return gradient.astype(jnp.bfloat16)


def block_kernel(n_images, n_texts, n_old, n_before, tiles, diagonal, where, jobs, *refs):
    refs = list(refs)
    take = lambda n: [refs.pop(0) for _ in range(n)]
    scalars = take(1)[0] if tiles else None
    images, texts, old, before = take(n_images), take(n_texts), take(n_old), take(n_before)
    if tiles:
        new, sums = take(2)
        factor = scalars[0] * LOG2E
        offset = scalars[1] * LOG2E
        totals = [jnp.zeros((8, TILE), jnp.float32) for _ in range(4)]
        for t, (i, j) in enumerate(tiles):
            scores = lax.dot_general(
                images[i][...], texts[j][...], (((1,), (1,)), ((), ())), preferred_element_type=jnp.float32
            )
            new[t] = pair_tile(scores, factor, offset, t == diagonal, totals)
        sums[0] = totals[0] + LN2 * totals[1]
        sums[1] = totals[2]
        sums[2] = totals[3]
        old = old + [new]
    for out, row, kind, index, over, base in jobs:
        total = None
        for k in over:
            a, t = where[(index, k) if kind == "image" else (k, index)]
            rows, contract = (texts[k], 1) if kind == "image" else (images[k], 0)
            term = lax.dot_general(
                old[a][t], rows[...], (((contract,), (0,)), ((), ())), preferred_element_type=jnp.float32
            )
            total = term if total is None else total + term
        total = SCALE * total
        place = pl.ds(row * TILE, TILE)
        refs[out][place, :] = total if base is None else total + before[base][place, :]


def block(scalars, images, texts, old, where, tiles=(), diagonal=None, jobs=(), outs=(), before=()):
    vmem = pl.BlockSpec(memory_space=pltpu.VMEM)
    head = [scalars] if tiles else []
    out_shape = [jax.ShapeDtypeStruct((n * TILE, 1152), jnp.float32) for n in outs]
    if tiles:
        out_shape = [
            jax.ShapeDtypeStruct((len(tiles), TILE, TILE), jnp.bfloat16),
            jax.ShapeDtypeStruct((3, 8, TILE), jnp.float32),
        ] + out_shape
    return pl.pallas_call(
        functools.partial(
            block_kernel,
            len(images),
            len(texts),
            len(old),
            len(before),
            tuple(tiles),
            diagonal,
            dict(where),
            tuple(jobs),
        ),
        in_specs=[pl.BlockSpec(memory_space=pltpu.SMEM)] * len(head)
        + [vmem] * (len(images) + len(texts) + len(old) + len(before)),
        out_specs=[vmem] * len(out_shape),
        out_shape=out_shape,
        compiler_params=pltpu.CompilerParams(vmem_limit_bytes=24 * 1024 * 1024),
        cost_estimate=pl.CostEstimate(flops=1, bytes_accessed=1, transcendentals=0),
    )(*head, *images, *texts, *old, *before)


def narrow(value):
    return value.astype(jnp.float16)


def wide(value):
    return value.astype(jnp.float32)


def per_device(picture_embedding, caption_embedding, logarithmic_scale_factor, offset_shift):
    rows = picture_embedding.shape[0]
    example_number = rows * 128
    (both,) = fence(jnp.concatenate([picture_embedding, caption_embedding], axis=0))
    unit32, inverse = normalize(both)
    unit = unit32.astype(jnp.bfloat16)
    image, text = unit[:rows], unit[rows:]
    temperature = jnp.exp(logarithmic_scale_factor[0])
    scalars = jnp.stack([temperature, offset_shift[0]])

    image_z, text_z = send(image, Z, EVEN), send(text, Z, ODD)
    i_own = jnp.concatenate([image, image_z], axis=0)
    t_own = jnp.concatenate([text, text_z], axis=0)

    where = {}

    def place(number, tiles):
        where.update({p: (number, t) for t, p in enumerate(tiles)})
        return tiles

    weights_z, sums_z = block(scalars, [i_own], [t_own], [], where, place(4, [(0, 0)]), 0)
    scalars, weights_z, sums_z, i_low, i_high, t_low, t_high, text_s, text_zs = fence(
        scalars,
        weights_z,
        sums_z,
        send(i_own, "x", UP),
        send(i_own, "x", DOWN),
        send(t_own, "y", UP),
        send(t_own, "y", DOWN),
        send(text, "c", SWAP),
        send(text_z, "c", SWAP),
    )
    s_own = jnp.concatenate([text_s, text_zs], axis=0)

    far = [
        send(i_low[:rows], "x", UP),
        send(i_high[rows:], "x", DOWN),
        send(t_low[:rows], "y", UP),
        send(t_high[rows:], "y", DOWN),
    ]
    s_near = send(jnp.concatenate([t_low, t_high], axis=0), "c", SWAP)
    near_images = [i_own, i_low, i_high]
    near_texts = [t_own, t_low, t_high, s_own]
    tiles_a = place(0, [(i, j) for j in range(4) for i in range(3) if (i, j) != (0, 0)])
    weights_a, sums_a = block(scalars, near_images, near_texts, [], where, tiles_a)
    weights_a, s_near = fence(weights_a, s_near)
    s_low, s_high = s_near[: 2 * rows], s_near[2 * rows :]
    near_texts = [t_own, t_low, t_high, s_own, s_low, s_high]
    tiles_b = place(1, [(i, j) for j in (4, 5) for i in range(3)])
    shared = [(0, n, "text", j, (0, 1, 2), None) for n, j in enumerate((4, 5, 3))]
    weights_b, sums_b, ps_near = block(
        scalars, near_images, near_texts, [weights_a], where, tiles_b, None, shared, [3]
    )
    *far, weights_a, weights_b, ps_near = fence(*far, weights_a, weights_b, ps_near)
    i_far = jnp.concatenate(far[:2], axis=0)
    t_far = jnp.concatenate(far[2:], axis=0)
    s_far = send(t_far, "c", SWAP)

    images = [i_own, i_low, i_high, i_far]
    texts = [t_own, t_low, t_high, s_own, s_low, s_high, t_far]
    weights = [weights_a, weights_b]
    tiles_c = place(2, [(3, j) for j in range(7)] + [(i, 6) for i in range(3)])
    weights_c, sums_c, pi_far, pt_far = block(
        scalars,
        images,
        texts,
        weights,
        where,
        tiles_c,
        None,
        [(0, 0, "image", 3, tuple(range(7)), None), (1, 0, "text", 6, (0, 1, 2, 3), None)],
        [1, 1],
    )
    weights_c, s_far = fence(weights_c, s_far)
    texts = texts + [s_far]
    tiles_d = place(3, [(i, 7) for i in range(4)])
    weights_d, sums_d, ps_far = block(
        scalars, images, texts, weights + [weights_c], where, tiles_d, None, [(0, 0, "text", 7, (0, 1, 2, 3), None)], [1]
    )
    weights = [weights_a, weights_b, weights_c, weights_d, weights_z]

    value = jnp.sum(sums_z + sums_a + sums_b + sums_c + sums_d, axis=(1, 2)).reshape(1, 3)
    *weights, ps_far, value = fence(*weights, narrow(ps_far), value)
    ps_far = send(ps_far, "c", SWAP)
    value = value + send(value, "c", SWAP)
    pi_far, ps_near = block(
        None,
        images,
        texts,
        weights,
        where,
        jobs=[(0, 0, "image", 3, (7,), 0)] + [(1, n, "text", j, (3,), 1) for n, j in enumerate((4, 5, 3))],
        outs=[1, 3],
        before=[pi_far, ps_near],
    )
    ps_near = narrow(ps_near)
    pi_far = narrow(pi_far)
    pt_far = narrow(pt_far + wide(ps_far))
    pi_far, pt_far, ps_near, value, *weights = fence(pi_far, pt_far, ps_near, value, *weights)
    back = [
        send(pi_far[:rows], "x", DOWN),
        send(pi_far[rows:], "x", UP),
        send(pt_far[:rows], "y", DOWN),
        send(pt_far[rows:], "y", UP),
    ]
    ps_near = send(ps_near, "c", SWAP)
    pi_low, pi_high, pi_own, pt_low, pt_high, pt_own = block(
        None,
        images,
        texts,
        weights,
        where,
        jobs=[(n, 0, "image", i, tuple(range(8)), None) for n, i in enumerate((1, 2, 0))]
        + [(n + 3, 0, "text", j, (0, 1, 2, 3), None) for n, j in enumerate((1, 2, 0))],
        outs=[1] * 6,
    )
    pt_low = pt_low + wide(ps_near[: 2 * rows])
    pt_high = pt_high + wide(ps_near[2 * rows : 4 * rows])
    pt_own = pt_own + wide(ps_near[4 * rows :])
    *back, pi_low, pi_high, pi_own, pt_low, pt_high, pt_own = fence(
        *back, pi_low, pi_high, pi_own, pt_low, pt_high, pt_own
    )

    first, second = ((0, rows), (0, 0)), ((rows, 0), (0, 0))
    near = [
        narrow(pi_low + jnp.pad(wide(back[0]), first)),
        narrow(pi_high + jnp.pad(wide(back[1]), second)),
        narrow(pt_low + jnp.pad(wide(back[2]), first)),
        narrow(pt_high + jnp.pad(wide(back[3]), second)),
    ]
    *near, value = fence(*near, value)
    near = [
        send(near[0], "x", DOWN),
        send(near[1], "x", UP),
        send(near[2], "y", DOWN),
        send(near[3], "y", UP),
    ]
    for axis, pairs in ((Z, EVEN), (Z, ODD), ("x", EVEN)):
        value = value + send(value, axis, pairs)
    *near, pi_own, pt_own, value = fence(*near, pi_own, pt_own, value)
    pi_own = pi_own + wide(near[0]) + wide(near[1])
    pt_own = pt_own + wide(near[2]) + wide(near[3])

    last = [narrow(pi_own[rows:]), narrow(pt_own[rows:])]
    last = fence(*last)
    last = [send(last[0], Z, EVEN), send(last[1], Z, ODD)]
    value = value + send(value, "x", ODD)
    low, far, high = (send(value, "y", [(i, (i + step) % 4) for i in range(4)]) for step in (1, 2, 3))
    scale = temperature / SCALE
    image_gradient = projection(scale * (pi_own[:rows] + wide(last[0])), unit32[:rows], inverse[:rows])
    text_grad = projection(scale * (pt_own[:rows] + wide(last[1])), unit32[rows:], inverse[rows:])
    image_gradient, text_grad, value, low, far, high = fence(image_gradient, text_grad, value, low, far, high)
    value = (value + far) + (low + high)
    objective_results = value[0] * jnp.stack([jnp.float32(1.0), temperature, jnp.float32(1.0)]) / example_number
    return (image_gradient, text_grad, objective_results)


def solution(mesh):
    mesh = Mesh(mesh.devices.reshape(4, 4, 2, 2, 2), AXES)
    return jax.shard_map(
        per_device,
        mesh=mesh,
        in_specs=(P(AXES, None), P(AXES, None), P(), P()),
        out_specs=(P(AXES, None), P(AXES, None), P()),
        check_vma=False,
    )
```

```python
import functools

import jax
import jax.numpy as jnp
from jax import lax
from jax.experimental import pallas as pl
from jax.experimental.pallas import tpu as pltpu
from jax.sharding import Mesh, PartitionSpec as P

EPS = 1e-06
AXES = ("y", "x", "zh", "zl", "c")
Z = ("zh", "zl")
EVEN = [(0, 1), (1, 0), (2, 3), (3, 2)]
ODD = [(1, 2), (2, 1), (3, 0), (0, 3)]
UP = [(i, (i + 1) % 4) for i in range(4)]
DOWN = [(i, (i - 1) % 4) for i in range(4)]
SWAP = [(0, 1), (1, 0)]
SCALE = 4.0
TILE = 256
LOG2E = 1.4426950408889634
LN2 = 0.6931471805599453


def send(value, axis, pairs):
    return lax.ppermute(value, axis, pairs)


def fence(*values):
    return lax.optimization_barrier(values)


def normalize(embedding):
    widened = embedding.astype(jnp.float32)
    inverse = lax.rsqrt(jnp.sum(widened * widened, axis=1, keepdims=True) + EPS)
    return (widened * inverse, inverse)


def projection(total, unit_rows, inverse):
    radial = jnp.sum(total * unit_rows, axis=1, keepdims=True)
    return (total - radial * unit_rows) * inverse


def by_eight(value):
    return jnp.sum(value.reshape(value.shape[0] // 8, 8, value.shape[1]), axis=0)


def pair_tile(scores, factor, offset, diagonal, totals):
    logits = scores * factor + offset
    small = jnp.exp2(-jnp.abs(logits))
    inverse = pltpu.reciprocal(1.0 + small, approx=True)
    gradient = jnp.where(logits >= 0.0, 1.0, small) * inverse
    signed = logits
    if diagonal:
        row = lax.broadcasted_iota(jnp.int32, (TILE, TILE), 0)
        column = lax.broadcasted_iota(jnp.int32, (TILE, TILE), 1)
        matched = (row == column) & (row < TILE // 2)
        signed = jnp.where(matched, -logits, logits)
        gradient = jnp.where(matched, gradient - 1.0, gradient)
    product = small
    while product.shape[0] > 8:
        half = product.shape[0] // 2
        left, right = product[:half], product[half:]
        product = left + right + left * right
    totals[0] += jnp.log1p(product)
    totals[1] += by_eight(jnp.maximum(signed, 0.0))
    totals[2] += by_eight(gradient * scores)
    totals[3] += by_eight(gradient)
    return gradient.astype(jnp.bfloat16)


def block_kernel(n_images, n_texts, n_old, n_before, tiles, diagonal, where, jobs, *refs):
    refs = list(refs)
    take = lambda n: [refs.pop(0) for _ in range(n)]
    scalars = take(1)[0] if tiles else None
    images, texts, old, before = take(n_images), take(n_texts), take(n_old), take(n_before)
    if tiles:
        new, sums = take(2)
        factor = scalars[0] * LOG2E
        offset = scalars[1] * LOG2E
        totals = [jnp.zeros((8, TILE), jnp.float32) for _ in range(4)]
        for t, (i, j) in enumerate(tiles):
            scores = lax.dot_general(
                images[i][...], texts[j][...], (((1,), (1,)), ((), ())), preferred_element_type=jnp.float32
            )
            new[t] = pair_tile(scores, factor, offset, t == diagonal, totals)
        sums[0] = totals[0] + LN2 * totals[1]
        sums[1] = totals[2]
        sums[2] = totals[3]
        old = old + [new]
    for out, row, kind, index, over, base in jobs:
        total = None
        for k in over:
            a, t = where[(index, k) if kind == "image" else (k, index)]
            rows, contract = (texts[k], 1) if kind == "image" else (images[k], 0)
            term = lax.dot_general(
                old[a][t], rows[...], (((contract,), (0,)), ((), ())), preferred_element_type=jnp.float32
            )
            total = term if total is None else total + term
        total = SCALE * total
        place = pl.ds(row * TILE, TILE)
        refs[out][place, :] = total if base is None else total + before[base][place, :]


def block(scalars, images, texts, old, where, tiles=(), diagonal=None, jobs=(), outs=(), before=()):
    vmem = pl.BlockSpec(memory_space=pltpu.VMEM)
    head = [scalars] if tiles else []
    out_shape = [jax.ShapeDtypeStruct((n * TILE, 1152), jnp.float32) for n in outs]
    if tiles:
        out_shape = [
            jax.ShapeDtypeStruct((len(tiles), TILE, TILE), jnp.bfloat16),
            jax.ShapeDtypeStruct((3, 8, TILE), jnp.float32),
        ] + out_shape
    return pl.pallas_call(
        functools.partial(
            block_kernel,
            len(images),
            len(texts),
            len(old),
            len(before),
            tuple(tiles),
            diagonal,
            dict(where),
            tuple(jobs),
        ),
        in_specs=[pl.BlockSpec(memory_space=pltpu.SMEM)] * len(head)
        + [vmem] * (len(images) + len(texts) + len(old) + len(before)),
        out_specs=[vmem] * len(out_shape),
        out_shape=out_shape,
        compiler_params=pltpu.CompilerParams(vmem_limit_bytes=24 * 1024 * 1024),
        cost_estimate=pl.CostEstimate(flops=1, bytes_accessed=1, transcendentals=0),
    )(*head, *images, *texts, *old, *before)


def narrow(value):
    return value.astype(jnp.float16)


def wide(value):
    return value.astype(jnp.float32)


def per_device(picture_embedding, caption_embedding, logarithmic_scale_factor, offset_shift):
    rows = picture_embedding.shape[0]
    example_number = rows * 128
    (both,) = fence(jnp.concatenate([picture_embedding, caption_embedding], axis=0))
    unit32, inverse = normalize(both)
    unit = unit32.astype(jnp.bfloat16)
    image, text = unit[:rows], unit[rows:]
    temperature = jnp.exp(logarithmic_scale_factor[0])
    scalars = jnp.stack([temperature, offset_shift[0]])

    image_z, text_z = send(image, Z, EVEN), send(text, Z, ODD)
    i_own = jnp.concatenate([image, image_z], axis=0)
    t_own = jnp.concatenate([text, text_z], axis=0)

    where = {}

    def place(number, tiles):
        where.update({p: (number, t) for t, p in enumerate(tiles)})
        return tiles

    weights_z, sums_z = block(scalars, [i_own], [t_own], [], where, place(4, [(0, 0)]), 0)
    scalars, weights_z, sums_z, i_low, i_high, t_low, t_high, text_s, text_zs = fence(
        scalars,
        weights_z,
        sums_z,
        send(i_own, "x", UP),
        send(i_own, "x", DOWN),
        send(t_own, "y", UP),
        send(t_own, "y", DOWN),
        send(text, "c", SWAP),
        send(text_z, "c", SWAP),
    )
    s_own = jnp.concatenate([text_s, text_zs], axis=0)

    far = [
        send(i_low[:rows], "x", UP),
        send(i_high[rows:], "x", DOWN),
        send(t_low[:rows], "y", UP),
        send(t_high[rows:], "y", DOWN),
    ]
    s_near = send(jnp.concatenate([t_low, t_high], axis=0), "c", SWAP)
    near_images = [i_own, i_low, i_high]
    near_texts = [t_own, t_low, t_high, s_own]
    tiles_a = place(0, [(i, j) for j in range(4) for i in range(3) if (i, j) != (0, 0)])
    weights_a, sums_a = block(scalars, near_images, near_texts, [], where, tiles_a)
    weights_a, s_near = fence(weights_a, s_near)
    s_low, s_high = s_near[: 2 * rows], s_near[2 * rows :]
    near_texts = [t_own, t_low, t_high, s_own, s_low, s_high]
    tiles_b = place(1, [(i, j) for j in (4, 5) for i in range(3)])
    shared = [(0, n, "text", j, (0, 1, 2), None) for n, j in enumerate((4, 5, 3))]
    weights_b, sums_b, ps_near = block(
        scalars, near_images, near_texts, [weights_a], where, tiles_b, None, shared, [3]
    )
    *far, weights_a, weights_b, ps_near = fence(*far, weights_a, weights_b, ps_near)
    i_far = jnp.concatenate(far[:2], axis=0)
    t_far = jnp.concatenate(far[2:], axis=0)
    s_far = send(t_far, "c", SWAP)

    images = [i_own, i_low, i_high, i_far]
    texts = [t_own, t_low, t_high, s_own, s_low, s_high, t_far]
    weights = [weights_a, weights_b]
    tiles_c = place(2, [(3, j) for j in range(7)] + [(i, 6) for i in range(3)])
    weights_c, sums_c, pi_far = block(
        scalars,
        images,
        texts,
        weights,
        where,
        tiles_c,
        None,
        [(0, 0, "image", 3, tuple(range(7)), None)],
        [1],
    )
    weights_c, s_far = fence(weights_c, s_far)
    texts = texts + [s_far]
    tiles_d = place(3, [(i, 7) for i in range(4)])
    weights_d, sums_d, ps_far = block(
        scalars, images, texts, weights + [weights_c], where, tiles_d, None, [(0, 0, "text", 7, (0, 1, 2, 3), None)], [1]
    )
    weights = [weights_a, weights_b, weights_c, weights_d, weights_z]

    value = jnp.sum(sums_z + sums_a + sums_b + sums_c + sums_d, axis=(1, 2)).reshape(1, 3)
    *weights, ps_far, value = fence(*weights, narrow(ps_far), value)
    ps_far = send(ps_far, "c", SWAP)
    value = value + send(value, "c", SWAP)
    pi_far, ps_near, pt_far = block(
        None,
        images,
        texts,
        weights,
        where,
        jobs=[(0, 0, "image", 3, (7,), 0), (2, 0, "text", 6, (0, 1, 2, 3), None)]
        + [(1, n, "text", j, (3,), 1) for n, j in enumerate((4, 5, 3))],
        outs=[1, 3, 1],
        before=[pi_far, ps_near],
    )
    ps_near = narrow(ps_near)
    pi_far = narrow(pi_far)
    pt_far = narrow(pt_far + wide(ps_far))
    pi_far, pt_far, ps_near, value, *weights = fence(pi_far, pt_far, ps_near, value, *weights)
    back = [
        send(pi_far[:rows], "x", DOWN),
        send(pi_far[rows:], "x", UP),
        send(pt_far[:rows], "y", DOWN),
        send(pt_far[rows:], "y", UP),
    ]
    ps_near = send(ps_near, "c", SWAP)
    pi_low, pi_high, pi_own, pt_low, pt_high, pt_own = block(
        None,
        images,
        texts,
        weights,
        where,
        jobs=[(n, 0, "image", i, tuple(range(8)), None) for n, i in enumerate((1, 2, 0))]
        + [(n + 3, 0, "text", j, (0, 1, 2, 3), None) for n, j in enumerate((1, 2, 0))],
        outs=[1] * 6,
    )
    pt_low = pt_low + wide(ps_near[: 2 * rows])
    pt_high = pt_high + wide(ps_near[2 * rows : 4 * rows])
    pt_own = pt_own + wide(ps_near[4 * rows :])
    *back, pi_low, pi_high, pi_own, pt_low, pt_high, pt_own = fence(
        *back, pi_low, pi_high, pi_own, pt_low, pt_high, pt_own
    )

    first, second = ((0, rows), (0, 0)), ((rows, 0), (0, 0))
    near = [
        narrow(pi_low + jnp.pad(wide(back[0]), first)),
        narrow(pi_high + jnp.pad(wide(back[1]), second)),
        narrow(pt_low + jnp.pad(wide(back[2]), first)),
        narrow(pt_high + jnp.pad(wide(back[3]), second)),
    ]
    *near, value = fence(*near, value)
    near = [
        send(near[0], "x", DOWN),
        send(near[1], "x", UP),
        send(near[2], "y", DOWN),
        send(near[3], "y", UP),
    ]
    for axis, pairs in ((Z, EVEN), (Z, ODD), ("x", EVEN)):
        value = value + send(value, axis, pairs)
    *near, pi_own, pt_own, value = fence(*near, pi_own, pt_own, value)
    pi_own = pi_own + wide(near[0]) + wide(near[1])
    pt_own = pt_own + wide(near[2]) + wide(near[3])

    last = [narrow(pi_own[rows:]), narrow(pt_own[rows:])]
    last = fence(*last)
    last = [send(last[0], Z, EVEN), send(last[1], Z, ODD)]
    value = value + send(value, "x", ODD)
    low, far, high = (send(value, "y", [(i, (i + step) % 4) for i in range(4)]) for step in (1, 2, 3))
    scale = temperature / SCALE
    image_gradient = projection(scale * (pi_own[:rows] + wide(last[0])), unit32[:rows], inverse[:rows])
    text_grad = projection(scale * (pt_own[:rows] + wide(last[1])), unit32[rows:], inverse[rows:])
    image_gradient, text_grad, value, low, far, high = fence(image_gradient, text_grad, value, low, far, high)
    value = (value + far) + (low + high)
    objective_results = value[0] * jnp.stack([jnp.float32(1.0), temperature, jnp.float32(1.0)]) / example_number
    return (image_gradient, text_grad, objective_results)


def solution(mesh):
    mesh = Mesh(mesh.devices.reshape(4, 4, 2, 2, 2), AXES)
    return jax.shard_map(
        per_device,
        mesh=mesh,
        in_specs=(P(AXES, None), P(AXES, None), P(), P()),
        out_specs=(P(AXES, None), P(AXES, None), P()),
        check_vma=False,
    )
```
